512 devices in a mesh: orb: 16 (over x_lo, y, core), grid: 32 (over z, x_hi).
Axes of the slice: x: 4 (x_hi: 2, x_lo: 2; x = x_hi * 2 + x_lo), y: 4, z: 16, core: 2. Of those that a mesh axis runs over, the one named last changes fastest.
Arguments:
- coeffs: float32 [2, 16, 262144], P(None, 'orb', 'grid'), may hold values from -6 to 6
- gvec_map: int32 [262144], P('grid'), may hold values from 0 to 65535, as said below
- projectors: float32 [2, 32, 262144], P(None, None, 'grid'), may hold values from -0.0078125 to 0.0078125
- proj_atom: int32 [32], replicated, may hold values from 0 to 7, never falling along the last dimension, each value on 1 to 8 neighbouring positions
- proj_strength: float32 [32, 32], replicated, may hold values from -96 to 96
- v_ext: float32 [128, 128, 128], P('grid'), may hold values from -6 to 6
Outputs:
- h_orbitals: float32 [2, 16, 128, 128, 128], P(None, 'orb', 'grid')
The draws below stay inside these ranges and needn't reach their ends.
Inputs may be any that keep to these rules, and one draw needn't show every extreme that they name: `gvec_map`: entry i of each grid index's block of 8192 entries names a slot z * 512 + local column of that index, lying in slots 8 i to 8 i + 7.
All inputs are finite; a program needn't handle non-finite values.
Results may differ from the reference program's by a relative error of at most 0.0003.
Values sent between devices are 32-bit elements; how exact they have to be, the bound alone decides.
A program may use at most 128 MiB of HBM per device.

```python
import math
import jax
import jax.numpy as jnp
import numpy as np
from jax import lax

SIDE = 128
NPROJ = 32
ATOMS = 8
ORBS = 16
COLS_DEV = 512
NG_DEV = 8192
NG = 262144


def draw_gvec_map(key, part):
    key = jax.random.fold_in(key, 7)
    offsets = jax.random.randint(key, (NG,), 0, 8)
    position = jnp.arange(NG, dtype=jnp.int32)
    offsets = jnp.where(position == 0, 0, offsets)
    offsets = jnp.where(position == NG - 1, 7, offsets)
    return (8 * (position % NG_DEV) + offsets).astype(jnp.int32)


def level_of(own_key, shape, cuts, low, top_value):
    def one(dim, blocks):
        draws = jax.random.uniform(jax.random.fold_in(jax.random.fold_in(own_key, 6), dim), (blocks,), jnp.float32, low / len(cuts), top_value / len(cuts))
        return jnp.repeat(jnp.exp(draws), shape[dim] // blocks).reshape((-1,) + (1,) * (len(shape) - dim - 1))

    factor_of = one(*cuts[0])
    for cut in cuts[1:]:
        factor_of = factor_of * one(*cut)
    return factor_of


def profile(number_of, total, reach, skew):
    loads = [(1 << 20) // math.isqrt(rank ** skew) + 1 for rank in range(2, number_of + 1)]
    surplus, given = total - reach - (number_of - 1), [1] * (number_of - 1)
    while surplus > 0:
        movable = [i for i in range(number_of - 1) if given[i] < reach]
        whole, remaining = sum([loads[i] for i in movable]), surplus
        for i in movable:
            addition = min(reach - given[i], max(1, remaining * loads[i] // whole), surplus)
            given[i] = given[i] + addition
            surplus = surplus - addition
    return np.array([reach] + given)


def ragged_sizes(key, number_of, total, limit, lean):
    if number_of == 2:
        one = jax.random.randint(key, (), max(1, total - limit), min(limit, total - 1) + 1)
        return jnp.stack([one, total - one])
    sizes = jnp.asarray(profile(number_of, total, limit, lean), jnp.int32)
    twos = (number_of - 1) // 2
    source_of, receiver = sizes[1:1 + 2 * twos:2], sizes[2:2 + 2 * twos:2]
    slack = jnp.minimum(source_of - 1, limit - receiver)
    moved = jax.random.randint(jax.random.fold_in(key, 1), (twos,), 0, 1 << 20) % (slack + 1)
    sizes = sizes.at[1:1 + 2 * twos:2].set(source_of - moved).at[2:2 + 2 * twos:2].set(receiver + moved)
    return sizes[jax.random.permutation(jax.random.fold_in(key, 2), number_of)]


def scatter_about(rng, shape, scale, most, cuts=(), kind=jnp.bfloat16):
    array = jax.random.normal(rng, shape, jnp.float32) * scale
    if len(cuts) > 0:
        array = level_of(rng, shape, cuts, -0.22, 0.18) * array
    return jnp.clip(array, min=-most, max=most).astype(kind)


def setup_inputs(seed: int = 0) -> dict:
    key_list = jax.random.split(jax.random.key(seed), 7)
    return {
        "coeffs": scatter_about(key_list[0], (2, ORBS, NG), 1.0, 6.0, ((1, 16), (2, 32)), jnp.float32),
        "gvec_map": draw_gvec_map(jax.random.fold_in(key_list[6], 71), 0),
        "projectors": scatter_about(key_list[2], (2, NPROJ, NG), (2 * NG) ** -0.5, 0.0078125, ((2, 32),), jnp.float32),
        "proj_atom": jnp.searchsorted(jnp.cumsum(ragged_sizes(key_list[3], ATOMS, NPROJ, 2 * NPROJ // ATOMS, 1)), jnp.arange(NPROJ), side="right").astype(jnp.int32),
        "proj_strength": scatter_about(key_list[4], (NPROJ, NPROJ), 16.0, 96.0, (), jnp.float32),
        "v_ext": scatter_about(key_list[5], (SIDE, SIDE, SIDE), 1.0, 6.0, ((0, 32),), jnp.float32),
    }


HARTREE_COUPLING = 256.0


def frequency(indices, grid_side):
    return jnp.where(indices < grid_side // 2, indices, indices - grid_side).astype(jnp.float32)


def reference(coeffs, gvec_map, projectors, proj_atom, proj_strength, v_ext):
    highest = lax.Precision.HIGHEST
    position = jnp.arange(NG, dtype=jnp.int32)
    owner_dev = position // NG_DEV
    z_index = gvec_map // COLS_DEV
    column = owner_dev * COLS_DEV + gvec_map % COLS_DEV
    x_index = column // SIDE
    y_index = column % SIDE
    kinetic = 2.0 * (frequency(x_index, SIDE) ** 2 + frequency(y_index, SIDE) ** 2 + frequency(z_index, SIDE) ** 2) / (SIDE * SIDE)
    c_real, c_imag = coeffs[0], coeffs[1]
    p_real, p_imag = projectors[0], projectors[1]
    over_real = jnp.dot(c_real, p_real.T, precision=highest) + jnp.dot(c_imag, p_imag.T, precision=highest)
    over_imag = jnp.dot(c_imag, p_real.T, precision=highest) - jnp.dot(c_real, p_imag.T, precision=highest)
    coupling = jnp.where(proj_atom[:, None] == proj_atom[None, :], proj_strength, 0.0)
    applied_real = jnp.dot(over_real, coupling.T, precision=highest)
    applied_imag = jnp.dot(over_imag, coupling.T, precision=highest)
    t_real = kinetic * c_real + jnp.dot(applied_real, p_real, precision=highest) - jnp.dot(applied_imag, p_imag, precision=highest)
    t_imag = kinetic * c_imag + jnp.dot(applied_real, p_imag, precision=highest) + jnp.dot(applied_imag, p_real, precision=highest)

    def to_space(real_part, imag_part):
        values = lax.complex(real_part, imag_part)
        full_grid = jnp.zeros((SIDE, SIDE, SIDE), values.dtype).at[x_index, y_index, z_index].set(values)
        space_field = jnp.fft.ifftn(full_grid, norm="ortho")
        return jnp.transpose(space_field, (2, 0, 1))

    def add_density(running, parts):
        space_field = to_space(parts[0], parts[1])
        return running + jnp.real(space_field) ** 2 + jnp.imag(space_field) ** 2, None

    density, _ = lax.scan(add_density, jnp.zeros((SIDE, SIDE, SIDE), jnp.float32), (c_real, c_imag))
    spectrum = jnp.fft.fftn(density, norm="ortho")
    freq_axis = frequency(jnp.arange(SIDE, dtype=jnp.int32), SIDE)
    squared = freq_axis[:, None, None] ** 2 + freq_axis[None, :, None] ** 2 + freq_axis[None, None, :] ** 2
    kernel = jnp.where(squared > 0, HARTREE_COUPLING / jnp.maximum(squared, 1.0), 0.0)
    hartree = jnp.real(jnp.fft.ifftn(spectrum * kernel, norm="ortho")).astype(jnp.float32)
    potential = v_ext + hartree

    def apply_one(rows):
        wave_field = to_space(rows[0], rows[1])
        term_field = to_space(rows[2], rows[3])
        return jnp.stack([jnp.real(term_field) + potential * jnp.real(wave_field), jnp.imag(term_field) + potential * jnp.imag(wave_field)])

    result = lax.map(apply_one, (c_real, c_imag, t_real, t_imag))
    return jnp.transpose(result, (1, 0, 2, 3, 4))
```

```python
import functools

import jax
import jax.numpy as jnp
import ml_dtypes
import numpy as np
from jax import lax
from jax.experimental import pallas as pl
from jax.experimental.pallas import tpu as pltpu
from jax.sharding import PartitionSpec as P

HARTREE_COUPLING = 256.0
F32, BF16 = jnp.float32, jnp.bfloat16
MESH = pl.DeviceIdType.MESH
HIGHEST = lax.Precision.HIGHEST
PLANES = 4
ROWS = 8
TERM_AT = {"dens": (0,), "col": (1, 2), "pot": (3,)}


def halves(table):
    high = table.astype(ml_dtypes.bfloat16)
    low = (table - high.astype(np.float64)).astype(ml_dtypes.bfloat16)
    return np.stack([high, low])


def tables(side):
    grid = side // PLANES
    place = np.arange(side)

    def turn(first, second):
        angles = 2.0 * np.pi * ((first[:, None] * second[None, :]) % side) / side
        return np.cos(angles) / np.sqrt(side), np.sin(angles) / np.sqrt(side)

    expand = (np.arange(ROWS * side)[None, :] // ROWS == place[:, None]).astype(ml_dtypes.bfloat16)
    out_z = (PLANES * np.arange(grid)[None, :] + np.arange(PLANES)[:, None]).reshape(-1)
    in_z = (2 * np.arange(side // 2)[None, :] + np.arange(2)[:, None]).reshape(-1)
    cosine, sine = turn(out_z, in_z)
    z_table = np.block([[cosine, -sine], [sine, cosine]])
    cosine, sine = turn(place, place)
    y_table = np.block([[cosine, sine], [-sine, cosine]])
    cosine, sine = [t.reshape(side, grid, 1, PLANES) for t in turn(place, place)]
    x_table = np.concatenate(
        [np.concatenate([cosine, -sine], 2), np.concatenate([sine, cosine], 2)], 0
    ).reshape(2 * side, 2 * side)
    freq = (place + 1) // 2
    angles = 2.0 * np.pi * ((place[:, None] * freq[None, :]) % side) / side
    basis = np.where(place[None, :] % 2 == 1, np.cos(angles), np.sin(angles)) * np.sqrt(2.0 / side)
    basis[:, 0] = 1.0 / np.sqrt(side)
    basis[:, side - 1] = np.where(place % 2 == 0, 1.0, -1.0) / np.sqrt(side)
    spread = np.zeros((grid, ROWS, side))
    spread[:, :PLANES] = basis.reshape(grid, PLANES, side)
    spread = spread.reshape(grid * ROWS, side)
    real = np.concatenate([halves(basis), halves(basis.T)])
    return (
        expand,
        np.concatenate([halves(z_table), halves(y_table), halves(x_table)]),
        real,
        halves(spread.T),
        halves(spread),
    )


def split(values):
    high = values.astype(BF16)
    return high, (values - high.astype(F32)).astype(BF16)


def dot(left, right):
    return jnp.dot(left, right, preferred_element_type=F32)


def left_dot(table, first, values):
    high, low = split(values)
    return dot(table[first], high) + (dot(table[first], low) + dot(table[first + 1], high))


def right_dot(values, table, first):
    high, low = split(values)
    return dot(high, table[first]) + (dot(low, table[first]) + dot(high, table[first + 1]))


def turned_dot(left, right):
    return lax.dot_general(
        left, right, (((1,), (1,)), ((), ())), precision=HIGHEST, preferred_element_type=F32
    )


def kernel(
    side, grid, orbs,
    coef_hbm, gvec_hbm, atom_hbm, strength_hbm, expand_hbm, turn_hbm, real_hbm, zf_hbm, zb_hbm, proj_hbm, vext_hbm,
    out,
    coef, gvec, atom, strength, expand, turn, real, zfor, zback, proj, vext, proj_high, proj_low,
    mask, msg_c, msg_t, got_c, got_t, wave, dens_out, dens_in, col_out, col_in, ret_out, ret_in,
    pot_out, pot_in, dot_out, dot_in, nonlocal_rows,
    in_sem, send_c, recv_c, send_t, recv_t, send_dot, recv_dot, send_dens, recv_dens,
    send_col, recv_col, send_ret, recv_ret, send_pot, recv_pot,
):
    orb, place = lax.axis_index("orb"), lax.axis_index("grid")
    nproj = strength.shape[0]
    half = side // 2
    chunks, per = recv_c.shape[0], PLANES // recv_c.shape[0]
    term_chunks = recv_t.shape[0]

    loads = []
    for index, (source, target) in enumerate(
        [(gvec_hbm, gvec), (expand_hbm, expand), (coef_hbm, coef), (turn_hbm, turn), (proj_hbm, proj),
         (atom_hbm, atom), (strength_hbm, strength), (real_hbm, real), (zf_hbm, zfor), (zb_hbm, zback),
         (vext_hbm, vext)]
    ):
        loads.append(pltpu.make_async_copy(source, target, in_sem.at[index]))
        loads[-1].start()

    def over_grid(action):
        def step(k, carry):
            hop = jnp.where(k % 2 == 1, (k + 1) // 2, grid - k // 2)
            action(lax.rem(place + hop, grid))
            return carry

        lax.fori_loop(1, grid, step, 0)

    def over_orbs(action):
        def step(k, carry):
            action(lax.rem(orb + k, orbs))
            return carry

        lax.fori_loop(1, orbs, step, 0)

    def tile(index):
        return pl.ds(pl.multiple_of(index * ROWS, ROWS), ROWS)

    def push(source, target, send_sem, recv_sem, device):
        pltpu.make_async_remote_copy(
            src_ref=source, dst_ref=target, send_sem=send_sem, recv_sem=recv_sem,
            device_id=device, device_id_type=MESH,
        ).start()

    def settle(ref, sem):
        pltpu.make_async_copy(ref, ref, sem).wait()

    barrier = pltpu.get_barrier_semaphore()

    def greet(device):
        pl.semaphore_signal(barrier, inc=1, device_id=device, device_id_type=MESH)

    over_grid(lambda other: greet((orb, other)))
    over_orbs(lambda other: greet((other, place)))

    loads[0].wait()
    slot = gvec[...]
    iz, column = slot // (PLANES * side), slot % (PLANES * side)
    ix, iy = place * PLANES + column // side, column % side

    def frequency(index):
        return jnp.where(index < half, index, index - side).astype(F32)

    fx, fy, fz = frequency(ix), frequency(iy), frequency(iz)
    kinetic = 2.0 * (fx * fx + fy * fy + fz * fz) / (side * side)

    loads[1].wait()
    offset = (slot % ROWS).astype(F32).astype(BF16)
    wide_offset = dot(offset, expand[...])
    lane = lax.broadcasted_iota(jnp.int32, (half, ROWS * side), 1)
    mask[...] = jnp.where(wide_offset == (lane % ROWS).astype(F32), 1.0, 0.0)

    def fill_messages(real_part, imag_part, target):
        real_high, real_low = split(real_part)
        imag_high, imag_low = split(imag_part)
        wide = dot(jnp.concatenate([real_high, imag_high, real_low, imag_low], 0), expand[...])

        def slots(index):
            block = (wide[index * half:(index + 1) * half] * mask[...]).astype(BF16)
            return jnp.concatenate([block[:, : PLANES * side], block[:, PLANES * side:]], 0)

        high = jnp.concatenate([slots(0), slots(1)], 0)
        low = jnp.concatenate([slots(2), slots(3)], 0)
        sticks = dot(turn[0], high) + (dot(turn[0], low) + dot(turn[1], high))
        for x in range(PLANES):
            cols = slice(x * side, (x + 1) * side)
            lines = jnp.concatenate([sticks[:side, cols], sticks[side:, cols]], 1)
            lines = right_dot(lines, turn, 2)
            for plane in range(PLANES):
                for part in range(2):
                    target[plane, pl.ds(part * PLANES + x, grid, stride=ROWS), :] = lines[
                        plane * grid:(plane + 1) * grid, part * side:(part + 1) * side
                    ]

    loads[2].wait()
    loads[3].wait()
    fill_messages(coef[0], coef[1], msg_c)

    def send_planes(msg, got, chunk, send_sem, recv_sem):
        per = PLANES // send_sem.shape[0]
        planes = pl.ds(chunk * per, per)
        over_grid(
            lambda other: push(
                msg.at[planes, tile(other), :], got.at[planes, tile(place), :],
                send_sem.at[chunk], recv_sem.at[chunk], (orb, other),
            )
        )
        got[planes, tile(place), :] = msg[planes, tile(place), :]

    def all_but_one(ref, chunk, chunks):
        per = PLANES // chunks
        return ref.at[pl.ds(chunk * per, per), pl.ds(0, (grid - 1) * ROWS), :]

    pl.semaphore_wait(barrier, grid + orbs - 2)
    send_planes(msg_c, got_c, 0, send_c, recv_c)

    loads[4].wait()

    def gather(row, carry):
        over_real, over_imag = carry
        cols = pl.ds(pl.multiple_of(row * side, side), side)
        c_real, c_imag = coef[0, pl.ds(row, 1), :], coef[1, pl.ds(row, 1), :]
        p_real, p_imag = proj[:nproj, cols], proj[nproj:, cols]
        return (
            over_real + (c_real * p_real + c_imag * p_imag),
            over_imag + (c_imag * p_real - c_real * p_imag),
        )

    zeros = jnp.zeros((nproj, side), F32)
    over_real, over_imag = lax.fori_loop(0, half, gather, (zeros, zeros), unroll=4)
    ones = jnp.ones((ROWS, side), F32)
    dot_out[...] = jnp.zeros_like(dot_out)
    dot_out[0:1, 0:nproj] = turned_dot(ones, over_real)[0:1]
    dot_out[1:2, 0:nproj] = turned_dot(ones, over_imag)[0:1]
    power = jnp.sum(coef[0] * coef[0] + coef[1] * coef[1], axis=0, keepdims=True)
    dot_out[0:1, nproj:nproj + 1] = jnp.sum(power, axis=1, keepdims=True)
    over_grid(
        lambda other: push(dot_out, dot_in.at[place], send_dot, recv_dot, (orb, other))
    )
    dot_in[place] = dot_out[...]
    for chunk in range(1, chunks):
        send_planes(msg_c, got_c, chunk, send_c, recv_c)

    def halve(block, carry):
        cols = pl.ds(pl.multiple_of(block * ROWS * side, ROWS * side), ROWS * side)
        high, low = split(proj[:, cols])
        proj_high[:, cols] = high
        proj_low[:, cols] = low
        return carry

    lax.fori_loop(0, half // ROWS, halve, 0)

    loads[5].wait()
    loads[6].wait()
    settle(dot_in.at[pl.ds(0, grid - 1)], recv_dot)
    total = jnp.sum(dot_in[...], axis=0)
    mean = total[0:1, nproj:nproj + 1] / (side * side * side)
    row = lax.broadcasted_iota(jnp.int32, (ROWS, nproj), 0)
    both = jnp.where(row == 0, total[0:1, :nproj], total[1:2, :nproj])
    owner = jnp.broadcast_to(atom[...].astype(F32), (nproj, nproj))
    coupling = jnp.where(owner == owner.T, strength[...], 0.0)
    applied_high, applied_low = split(turned_dot(both, coupling))

    def spread(first):
        high, low = proj_high[first:first + nproj], proj_low[first:first + nproj]
        return dot(applied_high, high) + (dot(applied_high, low) + dot(applied_low, high))

    on_real, on_imag = spread(0), spread(nproj)
    term_real = on_real[0:1] - on_imag[1:2]
    term_imag = on_imag[0:1] + on_real[1:2]
    for r in range(half):
        nonlocal_rows[0, r:r + 1, :] = term_real[:, r * side:(r + 1) * side]
        nonlocal_rows[1, r:r + 1, :] = term_imag[:, r * side:(r + 1) * side]
    fill_messages(
        kinetic * coef[0] + nonlocal_rows[0], kinetic * coef[1] + nonlocal_rows[1], msg_t
    )

    def send_term(moment):
        for chunk in TERM_AT.get(moment, ()):
            send_planes(msg_t, got_t, chunk, send_t, recv_t)

    for index in (7, 8, 9, 10):
        loads[index].wait()
    for chunk in range(chunks):
        planes = range(chunk * per, (chunk + 1) * per)
        settle(all_but_one(got_c, chunk, chunks), recv_c.at[chunk])
        send_term("wave%d" % chunk)
        field = left_dot(turn, 4, jnp.concatenate([got_c[p] for p in planes], 1))
        density = field[:side] * field[:side] + field[side:] * field[side:] - mean
        for k, p in enumerate(planes):
            wave[0, p] = field[:side, k * side:(k + 1) * side]
            wave[1, p] = field[side:, k * side:(k + 1) * side]
        lines = jnp.concatenate([density[:, k * side:(k + 1) * side] for k in range(per)], 0)
        lines = right_dot(lines, real, 0)
        lines = jnp.concatenate([lines[k * side:(k + 1) * side] for k in range(per)], 1)
        modes = left_dot(real, 2, lines)
        for k, p in enumerate(planes):
            dens_out[p] = modes[:, k * side:(k + 1) * side]
        span = pl.ds(chunk * per, per)
        over_orbs(
            lambda other: push(
                dens_out.at[span, tile(other), :], dens_in.at[span, tile(orb), :],
                send_dens.at[chunk], recv_dens.at[chunk], (other, place),
            )
        )
        dens_in[span, tile(orb), :] = dens_out[span, tile(orb), :]

    send_term("dens")

    stride = grid // ROWS
    shift = lax.rem(orb, stride)
    my_row = place // stride
    is_owner = lax.rem(place, stride) == shift

    col_out[...] = jnp.zeros_like(col_out)
    for chunk in range(chunks):
        span = pl.ds(chunk * per, per)
        settle(dens_in.at[span, pl.ds(0, (orbs - 1) * ROWS), :], recv_dens.at[chunk])
        for p in range(chunk * per, (chunk + 1) * per):
            summed = dens_in[p, 0:ROWS, :]
            for o in range(1, orbs):
                summed = summed + dens_in[p, o * ROWS:(o + 1) * ROWS, :]
            col_out[pl.ds(p, ROWS, stride=ROWS), :] = summed

    def send_column(row_index, carry):
        target = row_index * stride + shift

        @pl.when(target != place)
        def _():
            push(
                col_out.at[tile(row_index), :], col_in.at[tile(place), :],
                send_col, recv_col, (orb, target),
            )

        return carry

    lax.fori_loop(0, ROWS, send_column, 0)
    send_term("col")

    @pl.when(is_owner)
    def _():
        col_in[tile(place), :] = col_out[tile(my_row), :]
        settle(col_in.at[pl.ds(0, (grid - 1) * ROWS), :], recv_col)
        kx = (orb * ROWS + my_row + 1) // 2
        kz = (lax.broadcasted_iota(jnp.int32, (side, side), 0) + 1) // 2
        ky = (lax.broadcasted_iota(jnp.int32, (side, side), 1) + 1) // 2
        squared = (kx * kx + ky * ky + kz * kz).astype(F32)
        coulomb = jnp.where(squared > 0, HARTREE_COUPLING / jnp.maximum(squared, 1.0), 0.0)
        spectrum = left_dot(zfor, 0, col_in[...]) * coulomb
        ret_out[...] = left_dot(zback, 0, spectrum)
        over_grid(
            lambda other: push(
                ret_out.at[tile(other), :], ret_in.at[tile(my_row), :],
                send_ret, recv_ret, (orb, other),
            )
        )
        ret_in[tile(my_row), :] = ret_out[tile(place), :]
        settle(ret_in.at[pl.ds(0, (ROWS - 1) * ROWS), :], recv_ret)
        settle(ret_out.at[pl.ds(0, (grid - 1) * ROWS), :], send_ret)
        settle(col_out.at[pl.ds(0, (ROWS - 1) * ROWS), :], send_col)

    @pl.when(jnp.logical_not(is_owner))
    def _():
        settle(ret_in, recv_ret)
        settle(col_out, send_col)

    for p in range(PLANES):
        pot_out[p] = ret_in[pl.ds(p, ROWS, stride=ROWS), :]
    over_orbs(
        lambda other: push(
            pot_out, pot_in.at[:, tile(orb), :], send_pot, recv_pot, (other, place)
        )
    )
    pot_in[:, tile(orb), :] = pot_out[...]
    send_term("pot")

    per_term = PLANES // term_chunks
    for chunk in range(term_chunks):
        planes = range(chunk * per_term, (chunk + 1) * per_term)
        settle(all_but_one(got_t, chunk, term_chunks), recv_t.at[chunk])
        field = left_dot(turn, 4, jnp.concatenate([got_t[p] for p in planes], 1))
        for k, p in enumerate(planes):
            out[0, 0, p] = field[:side, k * side:(k + 1) * side]
            out[1, 0, p] = field[side:, k * side:(k + 1) * side]

    settle(pot_in.at[:, pl.ds(0, (orbs - 1) * ROWS), :], recv_pot)
    lines = left_dot(real, 0, jnp.concatenate([pot_in[p] for p in range(PLANES)], 1))
    lines = jnp.concatenate([lines[:, p * side:(p + 1) * side] for p in range(PLANES)], 0)
    hartree = right_dot(lines, real, 2)
    for p in range(PLANES):
        potential = vext[p] + hartree[p * side:(p + 1) * side]
        out[0, 0, p] = out[0, 0, p] + potential * wave[0, p]
        out[1, 0, p] = out[1, 0, p] + potential * wave[1, p]

    for chunk in range(chunks):
        settle(all_but_one(msg_c, chunk, chunks), send_c.at[chunk])
        span = pl.ds(chunk * per, per)
        settle(dens_out.at[span, pl.ds(0, (orbs - 1) * ROWS), :], send_dens.at[chunk])
    for chunk in range(term_chunks):
        settle(all_but_one(msg_t, chunk, term_chunks), send_t.at[chunk])
    settle(dot_in.at[pl.ds(0, grid - 1)], send_dot)
    settle(pot_in.at[:, pl.ds(0, (orbs - 1) * ROWS), :], send_pot)


def body(grid, orbs, coeffs, gvec_map, projectors, proj_atom, proj_strength, v_ext):
    side = v_ext.shape[1]
    nproj = proj_strength.shape[0]
    count = coeffs.shape[2]
    chunks, term_chunks = 2, 4
    consts = [jnp.asarray(t) for t in tables(side)]
    dma = pltpu.SemaphoreType.DMA

    def vmem(*shape, dtype=F32):
        return pltpu.VMEM(shape, dtype)

    return pl.pallas_call(
        functools.partial(kernel, side, grid, orbs),
        out_shape=jax.ShapeDtypeStruct((2, 1) + v_ext.shape, F32),
        in_specs=[pl.BlockSpec(memory_space=pltpu.HBM)] * 11,
        out_specs=pl.BlockSpec(memory_space=pltpu.VMEM),
        scratch_shapes=[
            vmem(2, side // 2, side),
            vmem(side // 2, side, dtype=jnp.int32),
            vmem(1, nproj, dtype=jnp.int32),
            vmem(nproj, nproj),
        ]
        + [pltpu.VMEM(t.shape, t.dtype) for t in consts]
        + [
            vmem(2 * nproj, count),
            vmem(*v_ext.shape),
            vmem(2 * nproj, count, dtype=BF16),
            vmem(2 * nproj, count, dtype=BF16),
            vmem(side // 2, ROWS * side),
        ]
        + [vmem(PLANES, grid * ROWS, side)] * 4
        + [
            vmem(2, PLANES, side, side),
            vmem(PLANES, side, side),
            vmem(PLANES, side, side),
            vmem(ROWS * ROWS, side),
            vmem(grid * ROWS, side),
            vmem(grid * ROWS, side),
            vmem(ROWS * ROWS, side),
            vmem(PLANES, ROWS, side),
            vmem(PLANES, side, side),
            vmem(2, 128),
            vmem(grid, 2, 128),
            vmem(2, side // 2, side),
            dma((11,)),
            dma((chunks,)), dma((chunks,)), dma((term_chunks,)), dma((term_chunks,)),
            dma, dma,
            dma((chunks,)), dma((chunks,)),
            dma, dma, dma, dma, dma, dma,
        ],
        compiler_params=pltpu.CompilerParams(
            collective_id=0, has_side_effects=True, vmem_limit_bytes=60 << 20
        ),
        name="hamiltonian",
    )(
        coeffs.reshape(2, side // 2, side),
        gvec_map.reshape(side // 2, side),
        proj_atom.reshape(1, nproj),
        proj_strength,
        *consts,
        projectors.reshape(2 * nproj, count),
        v_ext,
    )


def solution(mesh):
    placed = (
        P(None, "orb", "grid"),
        P("grid"),
        P(None, None, "grid"),
        P(),
        P(),
        P("grid", None, None),
    )
    return jax.shard_map(
        functools.partial(body, mesh.shape["grid"], mesh.shape["orb"]),
        mesh=mesh,
        in_specs=placed,
        out_specs=P(None, "orb", "grid", None, None),
        check_vma=False,
    )
```

```python
import functools

import jax
import jax.numpy as jnp
import ml_dtypes
import numpy as np
from jax import lax
from jax.experimental import pallas as pl
from jax.experimental.pallas import tpu as pltpu
from jax.sharding import PartitionSpec as P

HARTREE_COUPLING = 256.0
F32, BF16 = jnp.float32, jnp.bfloat16
MESH = pl.DeviceIdType.MESH
HIGHEST = lax.Precision.HIGHEST
PLANES = 4
ROWS = 8
TERM_AT = {"dens": (0,), "col": (1,), "ret": (2, 3)}


def halves(table):
    high = table.astype(ml_dtypes.bfloat16)
    low = (table - high.astype(np.float64)).astype(ml_dtypes.bfloat16)
    return np.stack([high, low])


def tables(side):
    grid = side // PLANES
    place = np.arange(side)

    def turn(first, second):
        angles = 2.0 * np.pi * ((first[:, None] * second[None, :]) % side) / side
        return np.cos(angles) / np.sqrt(side), np.sin(angles) / np.sqrt(side)

    expand = (np.arange(ROWS * side)[None, :] // ROWS == place[:, None]).astype(ml_dtypes.bfloat16)
    out_z = (PLANES * np.arange(grid)[None, :] + np.arange(PLANES)[:, None]).reshape(-1)
    in_z = (2 * np.arange(side // 2)[None, :] + np.arange(2)[:, None]).reshape(-1)
    cosine, sine = turn(out_z, in_z)
    z_table = np.block([[cosine, -sine], [sine, cosine]])
    cosine, sine = turn(place, place)
    y_table = np.block([[cosine, sine], [-sine, cosine]])
    cosine, sine = [t.reshape(side, grid, 1, PLANES) for t in turn(place, place)]
    x_table = np.concatenate(
        [np.concatenate([cosine, -sine], 2), np.concatenate([sine, cosine], 2)], 0
    ).reshape(2 * side, 2 * side)
    freq = (place + 1) // 2
    angles = 2.0 * np.pi * ((place[:, None] * freq[None, :]) % side) / side
    basis = np.where(place[None, :] % 2 == 1, np.cos(angles), np.sin(angles)) * np.sqrt(2.0 / side)
    basis[:, 0] = 1.0 / np.sqrt(side)
    basis[:, side - 1] = np.where(place % 2 == 0, 1.0, -1.0) / np.sqrt(side)
    spread = np.zeros((grid, ROWS, side))
    spread[:, :PLANES] = basis.reshape(grid, PLANES, side)
    spread = spread.reshape(grid * ROWS, side)
    real = np.concatenate([halves(basis), halves(basis.T)])
    return (
        expand,
        np.concatenate([halves(z_table), halves(y_table), halves(x_table)]),
        real,
        halves(spread.T),
        halves(spread),
    )


def split(values):
    high = values.astype(BF16)
    return high, (values - high.astype(F32)).astype(BF16)


def dot(left, right):
    return jnp.dot(left, right, preferred_element_type=F32)


def left_dot(table, first, values):
    high, low = split(values)
    return dot(table[first], high) + (dot(table[first], low) + dot(table[first + 1], high))


def right_dot(values, table, first):
    high, low = split(values)
    return dot(high, table[first]) + (dot(low, table[first]) + dot(high, table[first + 1]))


def turned_dot(left, right):
    return lax.dot_general(
        left, right, (((1,), (1,)), ((), ())), precision=HIGHEST, preferred_element_type=F32
    )


def kernel(
    side, grid, orbs,
    coef_hbm, gvec_hbm, atom_hbm, strength_hbm, expand_hbm, turn_hbm, real_hbm, zf_hbm, zb_hbm, proj_hbm, vext_hbm,
    out,
    coef, gvec, atom, strength, expand, turn, real, zfor, zback, proj, vext, proj_high, proj_low,
    mask, msg_c, msg_t, got_c, got_t, wave, dens_out, dens_in, col_out, col_in, ret_out, ret_in,
    pot_out, pot_in, dot_out, dot_in, nonlocal_rows,
    in_sem, send_c, recv_c, send_t, recv_t, send_dot, recv_dot, send_dens, recv_dens,
    send_col, recv_col, send_ret, recv_ret, send_pot, recv_pot,
):
    orb, place = lax.axis_index("orb"), lax.axis_index("grid")
    nproj = strength.shape[0]
    half = side // 2
    chunks, per = recv_c.shape[0], PLANES // recv_c.shape[0]
    term_chunks = recv_t.shape[0]

    loads = []
    for index, (source, target) in enumerate(
        [(gvec_hbm, gvec), (expand_hbm, expand), (coef_hbm, coef), (turn_hbm, turn), (proj_hbm, proj),
         (atom_hbm, atom), (strength_hbm, strength), (real_hbm, real), (zf_hbm, zfor), (zb_hbm, zback),
         (vext_hbm, vext)]
    ):
        loads.append(pltpu.make_async_copy(source, target, in_sem.at[index]))
        loads[-1].start()

    def over_grid(action):
        def step(k, carry):
            m = grid - k
            hop = jnp.where(m % 2 == 1, (m + 1) // 2, grid - m // 2)
            action(lax.rem(place + hop, grid))
            return carry

        lax.fori_loop(1, grid, step, 0)

    def over_orbs(action):
        def step(k, carry):
            action(lax.rem(orb + k, orbs))
            return carry

        lax.fori_loop(1, orbs, step, 0)

    def tile(index):
        return pl.ds(pl.multiple_of(index * ROWS, ROWS), ROWS)

    def push(source, target, send_sem, recv_sem, device):
        pltpu.make_async_remote_copy(
            src_ref=source, dst_ref=target, send_sem=send_sem, recv_sem=recv_sem,
            device_id=device, device_id_type=MESH,
        ).start()

    def settle(ref, sem):
        pltpu.make_async_copy(ref, ref, sem).wait()

    barrier = pltpu.get_barrier_semaphore()

    def greet(device):
        pl.semaphore_signal(barrier, inc=1, device_id=device, device_id_type=MESH)

    over_grid(lambda other: greet((orb, other)))
    over_orbs(lambda other: greet((other, place)))

    loads[0].wait()
    slot = gvec[...]
    iz, column = slot // (PLANES * side), slot % (PLANES * side)
    ix, iy = place * PLANES + column // side, column % side

    def frequency(index):
        return jnp.where(index < half, index, index - side).astype(F32)

    fx, fy, fz = frequency(ix), frequency(iy), frequency(iz)
    kinetic = 2.0 * (fx * fx + fy * fy + fz * fz) / (side * side)

    loads[1].wait()
    offset = (slot % ROWS).astype(F32).astype(BF16)
    wide_offset = dot(offset, expand[...])
    lane = lax.broadcasted_iota(jnp.int32, (half, ROWS * side), 1)
    mask[...] = jnp.where(wide_offset == (lane % ROWS).astype(F32), 1.0, 0.0)

    def fill_messages(real_part, imag_part, target):
        real_high, real_low = split(real_part)
        imag_high, imag_low = split(imag_part)
        wide = dot(jnp.concatenate([real_high, imag_high, real_low, imag_low], 0), expand[...])

        def slots(index):
            block = (wide[index * half:(index + 1) * half] * mask[...]).astype(BF16)
            return jnp.concatenate([block[:, : PLANES * side], block[:, PLANES * side:]], 0)

        high = jnp.concatenate([slots(0), slots(1)], 0)
        low = jnp.concatenate([slots(2), slots(3)], 0)
        sticks = dot(turn[0], high) + (dot(turn[0], low) + dot(turn[1], high))
        for x in range(PLANES):
            cols = slice(x * side, (x + 1) * side)
            lines = jnp.concatenate([sticks[:side, cols], sticks[side:, cols]], 1)
            lines = right_dot(lines, turn, 2)
            for plane in range(PLANES):
                for part in range(2):
                    target[plane, pl.ds(part * PLANES + x, grid, stride=ROWS), :] = lines[
                        plane * grid:(plane + 1) * grid, part * side:(part + 1) * side
                    ]

    loads[2].wait()
    loads[3].wait()
    fill_messages(coef[0], coef[1], msg_c)

    def send_planes(msg, got, chunk, send_sem, recv_sem):
        per = PLANES // send_sem.shape[0]
        planes = pl.ds(chunk * per, per)
        over_grid(
            lambda other: push(
                msg.at[planes, tile(other), :], got.at[planes, tile(place), :],
                send_sem.at[chunk], recv_sem.at[chunk], (orb, other),
            )
        )
        got[planes, tile(place), :] = msg[planes, tile(place), :]

    def all_but_one(ref, chunk, chunks):
        per = PLANES // chunks
        return ref.at[pl.ds(chunk * per, per), pl.ds(0, (grid - 1) * ROWS), :]

    loads[4].wait()

    def gather(row, carry):
        over_real, over_imag = carry
        cols = pl.ds(pl.multiple_of(row * side, side), side)
        c_real, c_imag = coef[0, pl.ds(row, 1), :], coef[1, pl.ds(row, 1), :]
        p_real, p_imag = proj[:nproj, cols], proj[nproj:, cols]
        return (
            over_real + (c_real * p_real + c_imag * p_imag),
            over_imag + (c_imag * p_real - c_real * p_imag),
        )

    zeros = jnp.zeros((nproj, side), F32)
    over_real, over_imag = lax.fori_loop(0, half, gather, (zeros, zeros), unroll=4)
    ones = jnp.ones((ROWS, side), F32)
    dot_out[...] = jnp.zeros_like(dot_out)
    dot_out[0:1, 0:nproj] = turned_dot(ones, over_real)[0:1]
    dot_out[1:2, 0:nproj] = turned_dot(ones, over_imag)[0:1]
    power = jnp.sum(coef[0] * coef[0] + coef[1] * coef[1], axis=0, keepdims=True)
    dot_out[0:1, nproj:nproj + 1] = jnp.sum(power, axis=1, keepdims=True)
    pl.semaphore_wait(barrier, grid + orbs - 2)
    over_grid(
        lambda other: push(dot_out, dot_in.at[place], send_dot, recv_dot, (orb, other))
    )
    dot_in[place] = dot_out[...]
    for chunk in range(chunks):
        send_planes(msg_c, got_c, chunk, send_c, recv_c)

    def halve(block, carry):
        cols = pl.ds(pl.multiple_of(block * ROWS * side, ROWS * side), ROWS * side)
        high, low = split(proj[:, cols])
        proj_high[:, cols] = high
        proj_low[:, cols] = low
        return carry

    lax.fori_loop(0, half // ROWS, halve, 0)

    loads[5].wait()
    loads[6].wait()
    settle(dot_in.at[pl.ds(0, grid - 1)], recv_dot)
    total = jnp.sum(dot_in[...], axis=0)
    mean = total[0:1, nproj:nproj + 1] / (side * side * side)
    row = lax.broadcasted_iota(jnp.int32, (ROWS, nproj), 0)
    both = jnp.where(row == 0, total[0:1, :nproj], total[1:2, :nproj])
    owner = jnp.broadcast_to(atom[...].astype(F32), (nproj, nproj))
    coupling = jnp.where(owner == owner.T, strength[...], 0.0)
    applied_high, applied_low = split(turned_dot(both, coupling))

    def spread(first):
        high, low = proj_high[first:first + nproj], proj_low[first:first + nproj]
        return dot(applied_high, high) + (dot(applied_high, low) + dot(applied_low, high))

    on_real, on_imag = spread(0), spread(nproj)
    term_real = on_real[0:1] - on_imag[1:2]
    term_imag = on_imag[0:1] + on_real[1:2]
    for r in range(half):
        nonlocal_rows[0, r:r + 1, :] = term_real[:, r * side:(r + 1) * side]
        nonlocal_rows[1, r:r + 1, :] = term_imag[:, r * side:(r + 1) * side]
    fill_messages(
        kinetic * coef[0] + nonlocal_rows[0], kinetic * coef[1] + nonlocal_rows[1], msg_t
    )

    def send_term(moment):
        for chunk in TERM_AT.get(moment, ()):
            send_planes(msg_t, got_t, chunk, send_t, recv_t)

    for index in (7, 8, 9, 10):
        loads[index].wait()
    for chunk in range(chunks):
        planes = range(chunk * per, (chunk + 1) * per)
        settle(all_but_one(got_c, chunk, chunks), recv_c.at[chunk])
        send_term("wave%d" % chunk)
        field = left_dot(turn, 4, jnp.concatenate([got_c[p] for p in planes], 1))
        density = field[:side] * field[:side] + field[side:] * field[side:] - mean
        for k, p in enumerate(planes):
            wave[0, p] = field[:side, k * side:(k + 1) * side]
            wave[1, p] = field[side:, k * side:(k + 1) * side]
        modes = left_dot(real, 2, density)
        for k, p in enumerate(planes):
            dens_out[p] = modes[:, k * side:(k + 1) * side]
        span = pl.ds(chunk * per, per)
        over_orbs(
            lambda other: push(
                dens_out.at[span, tile(other), :], dens_in.at[span, tile(orb), :],
                send_dens.at[chunk], recv_dens.at[chunk], (other, place),
            )
        )
        dens_in[span, tile(orb), :] = dens_out[span, tile(orb), :]

    send_term("dens")

    stride = grid // ROWS
    shift = lax.rem(orb, stride)
    my_row = place // stride
    is_owner = lax.rem(place, stride) == shift

    col_out[...] = jnp.zeros_like(col_out)
    sums = []
    for chunk in range(chunks):
        span = pl.ds(chunk * per, per)
        settle(dens_in.at[span, pl.ds(0, (orbs - 1) * ROWS), :], recv_dens.at[chunk])
        for p in range(chunk * per, (chunk + 1) * per):
            summed = dens_in[p, 0:ROWS, :]
            for o in range(1, orbs):
                summed = summed + dens_in[p, o * ROWS:(o + 1) * ROWS, :]
            sums.append(summed)
    modes = right_dot(jnp.concatenate(sums, 0), real, 0)
    for p in range(PLANES):
        col_out[pl.ds(p, ROWS, stride=ROWS), :] = modes[p * ROWS:(p + 1) * ROWS]

    def send_column(row_index, carry):
        target = row_index * stride + shift

        @pl.when(target != place)
        def _():
            push(
                col_out.at[tile(row_index), :], col_in.at[tile(place), :],
                send_col, recv_col, (orb, target),
            )

        return carry

    lax.fori_loop(0, ROWS, send_column, 0)
    send_term("col")

    @pl.when(is_owner)
    def _():
        col_in[tile(place), :] = col_out[tile(my_row), :]
        settle(col_in.at[pl.ds(0, (grid - 1) * ROWS), :], recv_col)
        kx = (orb * ROWS + my_row + 1) // 2
        kz = (lax.broadcasted_iota(jnp.int32, (side, side), 0) + 1) // 2
        ky = (lax.broadcasted_iota(jnp.int32, (side, side), 1) + 1) // 2
        squared = (kx * kx + ky * ky + kz * kz).astype(F32)
        coulomb = jnp.where(squared > 0, HARTREE_COUPLING / jnp.maximum(squared, 1.0), 0.0)
        spectrum = left_dot(zfor, 0, col_in[...]) * coulomb
        ret_out[...] = left_dot(zback, 0, spectrum)
        over_grid(
            lambda other: push(
                ret_out.at[tile(other), :], ret_in.at[tile(my_row), :],
                send_ret, recv_ret, (orb, other),
            )
        )
        ret_in[tile(my_row), :] = ret_out[tile(place), :]
        send_term("ret")
        settle(ret_in.at[pl.ds(0, (ROWS - 1) * ROWS), :], recv_ret)
        settle(ret_out.at[pl.ds(0, (grid - 1) * ROWS), :], send_ret)
        settle(col_out.at[pl.ds(0, (ROWS - 1) * ROWS), :], send_col)

    @pl.when(jnp.logical_not(is_owner))
    def _():
        send_term("ret")
        settle(ret_in, recv_ret)
        settle(col_out, send_col)

    rows = jnp.concatenate([ret_in[pl.ds(p, ROWS, stride=ROWS), :] for p in range(PLANES)], 0)
    rows = right_dot(rows, real, 2)
    for p in range(PLANES):
        pot_out[p] = rows[p * ROWS:(p + 1) * ROWS]
    over_orbs(
        lambda other: push(
            pot_out, pot_in.at[:, tile(orb), :], send_pot, recv_pot, (other, place)
        )
    )
    pot_in[:, tile(orb), :] = pot_out[...]
    send_term("pot")

    per_term = PLANES // term_chunks
    for chunk in range(term_chunks):
        planes = range(chunk * per_term, (chunk + 1) * per_term)
        settle(all_but_one(got_t, chunk, term_chunks), recv_t.at[chunk])
        field = left_dot(turn, 4, jnp.concatenate([got_t[p] for p in planes], 1))
        for k, p in enumerate(planes):
            out[0, 0, p] = field[:side, k * side:(k + 1) * side]
            out[1, 0, p] = field[side:, k * side:(k + 1) * side]

    settle(pot_in.at[:, pl.ds(0, (orbs - 1) * ROWS), :], recv_pot)
    hartree = left_dot(real, 0, jnp.concatenate([pot_in[p] for p in range(PLANES)], 1))
    for p in range(PLANES):
        potential = vext[p] + hartree[:, p * side:(p + 1) * side]
        out[0, 0, p] = out[0, 0, p] + potential * wave[0, p]
        out[1, 0, p] = out[1, 0, p] + potential * wave[1, p]

    for chunk in range(chunks):
        settle(all_but_one(msg_c, chunk, chunks), send_c.at[chunk])
        span = pl.ds(chunk * per, per)
        settle(dens_out.at[span, pl.ds(0, (orbs - 1) * ROWS), :], send_dens.at[chunk])
    for chunk in range(term_chunks):
        settle(all_but_one(msg_t, chunk, term_chunks), send_t.at[chunk])
    settle(dot_in.at[pl.ds(0, grid - 1)], send_dot)
    settle(pot_in.at[:, pl.ds(0, (orbs - 1) * ROWS), :], send_pot)


def body(grid, orbs, coeffs, gvec_map, projectors, proj_atom, proj_strength, v_ext):
    side = v_ext.shape[1]
    nproj = proj_strength.shape[0]
    count = coeffs.shape[2]
    chunks, term_chunks = 2, 4
    consts = [jnp.asarray(t) for t in tables(side)]
    dma = pltpu.SemaphoreType.DMA

    def vmem(*shape, dtype=F32):
        return pltpu.VMEM(shape, dtype)

    return pl.pallas_call(
        functools.partial(kernel, side, grid, orbs),
        out_shape=jax.ShapeDtypeStruct((2, 1) + v_ext.shape, F32),
        in_specs=[pl.BlockSpec(memory_space=pltpu.HBM)] * 11,
        out_specs=pl.BlockSpec(memory_space=pltpu.VMEM),
        scratch_shapes=[
            vmem(2, side // 2, side),
            vmem(side // 2, side, dtype=jnp.int32),
            vmem(1, nproj, dtype=jnp.int32),
            vmem(nproj, nproj),
        ]
        + [pltpu.VMEM(t.shape, t.dtype) for t in consts]
        + [
            vmem(2 * nproj, count),
            vmem(*v_ext.shape),
            vmem(2 * nproj, count, dtype=BF16),
            vmem(2 * nproj, count, dtype=BF16),
            vmem(side // 2, ROWS * side),
        ]
        + [vmem(PLANES, grid * ROWS, side)] * 4
        + [
            vmem(2, PLANES, side, side),
            vmem(PLANES, side, side),
            vmem(PLANES, side, side),
            vmem(ROWS * ROWS, side),
            vmem(grid * ROWS, side),
            vmem(grid * ROWS, side),
            vmem(ROWS * ROWS, side),
            vmem(PLANES, ROWS, side),
            vmem(PLANES, side, side),
            vmem(2, 128),
            vmem(grid, 2, 128),
            vmem(2, side // 2, side),
            dma((11,)),
            dma((chunks,)), dma((chunks,)), dma((term_chunks,)), dma((term_chunks,)),
            dma, dma,
            dma((chunks,)), dma((chunks,)),
            dma, dma, dma, dma, dma, dma,
        ],
        compiler_params=pltpu.CompilerParams(
            collective_id=0, has_side_effects=True, vmem_limit_bytes=60 << 20
        ),
        name="hamiltonian",
    )(
        coeffs.reshape(2, side // 2, side),
        gvec_map.reshape(side // 2, side),
        proj_atom.reshape(1, nproj),
        proj_strength,
        *consts,
        projectors.reshape(2 * nproj, count),
        v_ext,
    )


def solution(mesh):
    placed = (
        P(None, "orb", "grid"),
        P("grid"),
        P(None, None, "grid"),
        P(),
        P(),
        P("grid", None, None),
    )
    return jax.shard_map(
        functools.partial(body, mesh.shape["grid"], mesh.shape["orb"]),
        mesh=mesh,
        in_specs=placed,
        out_specs=P(None, "orb", "grid", None, None),
        check_vma=False,
    )
```

```python
import functools

import jax
import jax.numpy as jnp
import ml_dtypes
import numpy as np
from jax import lax
from jax.experimental import pallas as pl
from jax.experimental.pallas import tpu as pltpu
from jax.sharding import PartitionSpec as P

HARTREE_COUPLING = 256.0
F32, BF16 = jnp.float32, jnp.bfloat16
MESH = pl.DeviceIdType.MESH
HIGHEST = lax.Precision.HIGHEST
PLANES = 4
ROWS = 8
TERM_AT = {"dens": (0,), "col": (1,), "idle": (2, 3), "ret": (2, 3)}


def halves(table):
    high = table.astype(ml_dtypes.bfloat16)
    low = (table - high.astype(np.float64)).astype(ml_dtypes.bfloat16)
    return np.stack([high, low])


def tables(side):
    grid = side // PLANES
    place = np.arange(side)

    def turn(first, second):
        angles = 2.0 * np.pi * ((first[:, None] * second[None, :]) % side) / side
        return np.cos(angles) / np.sqrt(side), np.sin(angles) / np.sqrt(side)

    expand = (np.arange(ROWS * side)[None, :] // ROWS == place[:, None]).astype(ml_dtypes.bfloat16)
    out_z = (PLANES * np.arange(grid)[None, :] + np.arange(PLANES)[:, None]).reshape(-1)
    in_z = (2 * np.arange(side // 2)[None, :] + np.arange(2)[:, None]).reshape(-1)
    cosine, sine = turn(out_z, in_z)
    z_table = np.block([[cosine, -sine], [sine, cosine]])
    cosine, sine = turn(place, place)
    y_table = np.block([[cosine, sine], [-sine, cosine]])
    cosine, sine = [t.reshape(side, grid, 1, PLANES) for t in turn(place, place)]
    x_table = np.concatenate(
        [np.concatenate([cosine, -sine], 2), np.concatenate([sine, cosine], 2)], 0
    ).reshape(2 * side, 2 * side)
    freq = (place + 1) // 2
    angles = 2.0 * np.pi * ((place[:, None] * freq[None, :]) % side) / side
    basis = np.where(place[None, :] % 2 == 1, np.cos(angles), np.sin(angles)) * np.sqrt(2.0 / side)
    basis[:, 0] = 1.0 / np.sqrt(side)
    basis[:, side - 1] = np.where(place % 2 == 0, 1.0, -1.0) / np.sqrt(side)
    spread = np.zeros((grid, ROWS, side))
    spread[:, :PLANES] = basis.reshape(grid, PLANES, side)
    spread = spread.reshape(grid * ROWS, side)
    real = np.concatenate([halves(basis), halves(basis.T)])
    return (
        expand,
        np.concatenate([halves(z_table), halves(y_table), halves(x_table)]),
        real,
        halves(spread.T),
        halves(spread),
    )


def split(values):
    high = values.astype(BF16)
    return high, (values - high.astype(F32)).astype(BF16)


def dot(left, right):
    return jnp.dot(left, right, preferred_element_type=F32)


def left_dot(table, first, values):
    high, low = split(values)
    return dot(table[first], high) + (dot(table[first], low) + dot(table[first + 1], high))


def right_dot(values, table, first):
    high, low = split(values)
    return dot(high, table[first]) + (dot(low, table[first]) + dot(high, table[first + 1]))


def turned_dot(left, right):
    return lax.dot_general(
        left, right, (((1,), (1,)), ((), ())), precision=HIGHEST, preferred_element_type=F32
    )


def kernel(
    side, grid, orbs,
    coef_hbm, gvec_hbm, atom_hbm, strength_hbm, expand_hbm, turn_hbm, real_hbm, zf_hbm, zb_hbm, proj_hbm, vext_hbm,
    out,
    coef, gvec, atom, strength, expand, turn, real, zfor, zback, proj, vext, proj_high, proj_low,
    mask, msg_c, msg_t, got_c, got_t, wave, dens_out, dens_in, col_out, col_in, ret_out, ret_in,
    pot_out, pot_in, dot_out, dot_in, nonlocal_rows,
    in_sem, send_c, recv_c, send_t, recv_t, send_dot, recv_dot, send_dens, recv_dens,
    send_col, recv_col, send_ret, recv_ret, send_pot, recv_pot,
):
    orb, place = lax.axis_index("orb"), lax.axis_index("grid")
    nproj = strength.shape[0]
    half = side // 2
    chunks, per = recv_c.shape[0], PLANES // recv_c.shape[0]
    term_chunks = recv_t.shape[0]

    loads = []
    for index, (source, target) in enumerate(
        [(gvec_hbm, gvec), (expand_hbm, expand), (coef_hbm, coef), (turn_hbm, turn), (proj_hbm, proj),
         (atom_hbm, atom), (strength_hbm, strength), (real_hbm, real), (zf_hbm, zfor), (zb_hbm, zback),
         (vext_hbm, vext)]
    ):
        loads.append(pltpu.make_async_copy(source, target, in_sem.at[index]))
        loads[-1].start()

    def over_grid(action):
        def step(k, carry):
            m = grid - k
            hop = jnp.where(m % 2 == 1, (m + 1) // 2, grid - m // 2)
            action(lax.rem(place + hop, grid))
            return carry

        lax.fori_loop(1, grid, step, 0)

    def over_orbs(action):
        def step(k, carry):
            action(lax.rem(orb + k, orbs))
            return carry

        lax.fori_loop(1, orbs, step, 0)

    def tile(index):
        return pl.ds(pl.multiple_of(index * ROWS, ROWS), ROWS)

    def planes_of(index):
        return pl.ds(pl.multiple_of(index * ROWS, ROWS), PLANES)

    def push(source, target, send_sem, recv_sem, device):
        pltpu.make_async_remote_copy(
            src_ref=source, dst_ref=target, send_sem=send_sem, recv_sem=recv_sem,
            device_id=device, device_id_type=MESH,
        ).start()

    def settle(ref, sem):
        pltpu.make_async_copy(ref, ref, sem).wait()

    def settle_rows(count, sem):
        settle(col_in.at[pl.ds(0, count), :], sem)

    col_in[...] = jnp.zeros_like(col_in)
    barrier = pltpu.get_barrier_semaphore()

    def greet(device):
        pl.semaphore_signal(barrier, inc=1, device_id=device, device_id_type=MESH)

    over_grid(lambda other: greet((orb, other)))
    over_orbs(lambda other: greet((other, place)))

    loads[0].wait()
    slot = gvec[...]
    iz, column = slot // (PLANES * side), slot % (PLANES * side)
    ix, iy = place * PLANES + column // side, column % side

    def frequency(index):
        return jnp.where(index < half, index, index - side).astype(F32)

    fx, fy, fz = frequency(ix), frequency(iy), frequency(iz)
    kinetic = 2.0 * (fx * fx + fy * fy + fz * fz) / (side * side)

    loads[1].wait()
    offset = (slot % ROWS).astype(F32).astype(BF16)
    wide_offset = dot(offset, expand[...])
    lane = lax.broadcasted_iota(jnp.int32, (half, ROWS * side), 1)
    mask[...] = jnp.where(wide_offset == (lane % ROWS).astype(F32), 1.0, 0.0)

    def fill_messages(real_part, imag_part, target):
        real_high, real_low = split(real_part)
        imag_high, imag_low = split(imag_part)
        wide = dot(jnp.concatenate([real_high, imag_high, real_low, imag_low], 0), expand[...])

        def slots(index):
            block = (wide[index * half:(index + 1) * half] * mask[...]).astype(BF16)
            return jnp.concatenate([block[:, : PLANES * side], block[:, PLANES * side:]], 0)

        high = jnp.concatenate([slots(0), slots(1)], 0)
        low = jnp.concatenate([slots(2), slots(3)], 0)
        sticks = dot(turn[0], high) + (dot(turn[0], low) + dot(turn[1], high))
        for x in range(PLANES):
            cols = slice(x * side, (x + 1) * side)
            lines = jnp.concatenate([sticks[:side, cols], sticks[side:, cols]], 1)
            lines = right_dot(lines, turn, 2)
            for plane in range(PLANES):
                for part in range(2):
                    target[plane, pl.ds(part * PLANES + x, grid, stride=ROWS), :] = lines[
                        plane * grid:(plane + 1) * grid, part * side:(part + 1) * side
                    ]

    loads[2].wait()
    loads[3].wait()
    fill_messages(coef[0], coef[1], msg_c)

    def send_planes(msg, got, chunk, send_sem, recv_sem):
        per = PLANES // send_sem.shape[0]
        planes = pl.ds(chunk * per, per)
        over_grid(
            lambda other: push(
                msg.at[planes, tile(other), :], got.at[planes, tile(place), :],
                send_sem.at[chunk], recv_sem.at[chunk], (orb, other),
            )
        )
        got[planes, tile(place), :] = msg[planes, tile(place), :]

    def all_but_one(ref, chunk, chunks):
        per = PLANES // chunks
        return ref.at[pl.ds(chunk * per, per), pl.ds(0, (grid - 1) * ROWS), :]

    loads[4].wait()

    def gather(row, carry):
        over_real, over_imag = carry
        cols = pl.ds(pl.multiple_of(row * side, side), side)
        c_real, c_imag = coef[0, pl.ds(row, 1), :], coef[1, pl.ds(row, 1), :]
        p_real, p_imag = proj[:nproj, cols], proj[nproj:, cols]
        return (
            over_real + (c_real * p_real + c_imag * p_imag),
            over_imag + (c_imag * p_real - c_real * p_imag),
        )

    zeros = jnp.zeros((nproj, side), F32)
    over_real, over_imag = lax.fori_loop(0, half, gather, (zeros, zeros), unroll=4)
    ones = jnp.ones((ROWS, side), F32)
    dot_out[...] = jnp.zeros_like(dot_out)
    dot_out[0:1, 0:nproj] = turned_dot(ones, over_real)[0:1]
    dot_out[1:2, 0:nproj] = turned_dot(ones, over_imag)[0:1]
    power = jnp.sum(coef[0] * coef[0] + coef[1] * coef[1], axis=0, keepdims=True)
    dot_out[0:1, nproj:nproj + 1] = jnp.sum(power, axis=1, keepdims=True)
    pl.semaphore_wait(barrier, grid + orbs - 2)
    over_grid(
        lambda other: push(dot_out, dot_in.at[place], send_dot, recv_dot, (orb, other))
    )
    dot_in[place] = dot_out[...]
    for chunk in range(chunks):
        send_planes(msg_c, got_c, chunk, send_c, recv_c)

    def halve(block, carry):
        cols = pl.ds(pl.multiple_of(block * ROWS * side, ROWS * side), ROWS * side)
        high, low = split(proj[:, cols])
        proj_high[:, cols] = high
        proj_low[:, cols] = low
        return carry

    lax.fori_loop(0, half // ROWS, halve, 0)

    loads[5].wait()
    loads[6].wait()
    settle(dot_in.at[pl.ds(0, grid - 1)], recv_dot)
    total = jnp.sum(dot_in[...], axis=0)
    mean = total[0:1, nproj:nproj + 1] / (side * side * side)
    row = lax.broadcasted_iota(jnp.int32, (ROWS, nproj), 0)
    both = jnp.where(row == 0, total[0:1, :nproj], total[1:2, :nproj])
    owner = jnp.broadcast_to(atom[...].astype(F32), (nproj, nproj))
    coupling = jnp.where(owner == owner.T, strength[...], 0.0)
    applied_high, applied_low = split(turned_dot(both, coupling))

    def spread(first):
        high, low = proj_high[first:first + nproj], proj_low[first:first + nproj]
        return dot(applied_high, high) + (dot(applied_high, low) + dot(applied_low, high))

    on_real, on_imag = spread(0), spread(nproj)
    term_real = on_real[0:1] - on_imag[1:2]
    term_imag = on_imag[0:1] + on_real[1:2]
    for r in range(half):
        nonlocal_rows[0, r:r + 1, :] = term_real[:, r * side:(r + 1) * side]
        nonlocal_rows[1, r:r + 1, :] = term_imag[:, r * side:(r + 1) * side]
    fill_messages(
        kinetic * coef[0] + nonlocal_rows[0], kinetic * coef[1] + nonlocal_rows[1], msg_t
    )

    def send_term(moment):
        for chunk in TERM_AT.get(moment, ()):
            send_planes(msg_t, got_t, chunk, send_t, recv_t)

    for index in (7, 8, 9, 10):
        loads[index].wait()
    for chunk in range(chunks):
        planes = range(chunk * per, (chunk + 1) * per)
        settle(all_but_one(got_c, chunk, chunks), recv_c.at[chunk])
        send_term("wave%d" % chunk)
        field = left_dot(turn, 4, jnp.concatenate([got_c[p] for p in planes], 1))
        density = field[:side] * field[:side] + field[side:] * field[side:] - mean
        for k, p in enumerate(planes):
            wave[0, p] = field[:side, k * side:(k + 1) * side]
            wave[1, p] = field[side:, k * side:(k + 1) * side]
        modes = left_dot(real, 2, density)
        for k, p in enumerate(planes):
            dens_out[p] = modes[:, k * side:(k + 1) * side]
        span = pl.ds(chunk * per, per)
        over_orbs(
            lambda other: push(
                dens_out.at[span, tile(other), :], dens_in.at[span, tile(orb), :],
                send_dens.at[chunk], recv_dens.at[chunk], (other, place),
            )
        )
        dens_in[span, tile(orb), :] = dens_out[span, tile(orb), :]

    send_term("dens")

    stride = grid // ROWS
    shift = lax.rem(orb, stride)
    my_row = place // stride
    is_owner = lax.rem(place, stride) == shift

    col_out[...] = jnp.zeros_like(col_out)
    sums = []
    for chunk in range(chunks):
        span = pl.ds(chunk * per, per)
        settle(dens_in.at[span, pl.ds(0, (orbs - 1) * ROWS), :], recv_dens.at[chunk])
        for p in range(chunk * per, (chunk + 1) * per):
            summed = dens_in[p, 0:ROWS, :]
            for o in range(1, orbs):
                summed = summed + dens_in[p, o * ROWS:(o + 1) * ROWS, :]
            sums.append(summed)
    modes = right_dot(jnp.concatenate(sums, 0), real, 0)
    for p in range(PLANES):
        col_out[pl.ds(p, ROWS, stride=ROWS), :] = modes[p * ROWS:(p + 1) * ROWS]

    def send_column(row_index, carry):
        target = row_index * stride + shift

        @pl.when(target != place)
        def _():
            push(
                col_out.at[planes_of(row_index), :], col_in.at[planes_of(place), :],
                send_col, recv_col, (orb, target),
            )

        return carry

    lax.fori_loop(0, ROWS, send_column, 0)
    send_term("col")

    @pl.when(is_owner)
    def _():
        col_in[tile(place), :] = col_out[tile(my_row), :]
        settle_rows((grid - 1) * PLANES, recv_col)
        kx = (orb * ROWS + my_row + 1) // 2
        kz = (lax.broadcasted_iota(jnp.int32, (side, side), 0) + 1) // 2
        ky = (lax.broadcasted_iota(jnp.int32, (side, side), 1) + 1) // 2
        squared = (kx * kx + ky * ky + kz * kz).astype(F32)
        coulomb = jnp.where(squared > 0, HARTREE_COUPLING / jnp.maximum(squared, 1.0), 0.0)
        spectrum = left_dot(zfor, 0, col_in[...]) * coulomb
        ret_out[...] = left_dot(zback, 0, spectrum)
        over_grid(
            lambda other: push(
                ret_out.at[planes_of(other), :], ret_in.at[planes_of(my_row), :],
                send_ret, recv_ret, (orb, other),
            )
        )
        ret_in[tile(my_row), :] = ret_out[tile(place), :]
        send_term("ret")
        settle_rows((ROWS - 1) * PLANES, recv_ret)
        settle_rows((grid - 1) * PLANES, send_ret)
        settle_rows((ROWS - 1) * PLANES, send_col)

    @pl.when(jnp.logical_not(is_owner))
    def _():
        send_term("idle")
        settle_rows(ROWS * PLANES, recv_ret)
        settle_rows(ROWS * PLANES, send_col)

    rows = jnp.concatenate([ret_in[pl.ds(p, ROWS, stride=ROWS), :] for p in range(PLANES)], 0)
    rows = right_dot(rows, real, 2)
    for p in range(PLANES):
        pot_out[p] = rows[p * ROWS:(p + 1) * ROWS]
    over_orbs(
        lambda other: push(
            pot_out, pot_in.at[:, tile(orb), :], send_pot, recv_pot, (other, place)
        )
    )
    pot_in[:, tile(orb), :] = pot_out[...]
    send_term("pot")

    per_term = PLANES // term_chunks
    for chunk in range(term_chunks):
        planes = range(chunk * per_term, (chunk + 1) * per_term)
        settle(all_but_one(got_t, chunk, term_chunks), recv_t.at[chunk])
        field = left_dot(turn, 4, jnp.concatenate([got_t[p] for p in planes], 1))
        for k, p in enumerate(planes):
            out[0, 0, p] = field[:side, k * side:(k + 1) * side]
            out[1, 0, p] = field[side:, k * side:(k + 1) * side]

    settle(pot_in.at[:, pl.ds(0, (orbs - 1) * ROWS), :], recv_pot)
    hartree = left_dot(real, 0, jnp.concatenate([pot_in[p] for p in range(PLANES)], 1))
    for p in range(PLANES):
        potential = vext[p] + hartree[:, p * side:(p + 1) * side]
        out[0, 0, p] = out[0, 0, p] + potential * wave[0, p]
        out[1, 0, p] = out[1, 0, p] + potential * wave[1, p]

    for chunk in range(chunks):
        settle(all_but_one(msg_c, chunk, chunks), send_c.at[chunk])
        span = pl.ds(chunk * per, per)
        settle(dens_out.at[span, pl.ds(0, (orbs - 1) * ROWS), :], send_dens.at[chunk])
    for chunk in range(term_chunks):
        settle(all_but_one(msg_t, chunk, term_chunks), send_t.at[chunk])
    settle(dot_in.at[pl.ds(0, grid - 1)], send_dot)
    settle(pot_in.at[:, pl.ds(0, (orbs - 1) * ROWS), :], send_pot)


def body(grid, orbs, coeffs, gvec_map, projectors, proj_atom, proj_strength, v_ext):
    side = v_ext.shape[1]
    nproj = proj_strength.shape[0]
    count = coeffs.shape[2]
    chunks, term_chunks = 2, 4
    consts = [jnp.asarray(t) for t in tables(side)]
    dma = pltpu.SemaphoreType.DMA

    def vmem(*shape, dtype=F32):
        return pltpu.VMEM(shape, dtype)

    operands = [
        coeffs.reshape(2, side // 2, side),
        gvec_map.reshape(side // 2, side),
        proj_atom.reshape(1, nproj),
        proj_strength,
        *consts,
        projectors.reshape(2 * nproj, count),
        v_ext,
    ]
    return pl.pallas_call(
        functools.partial(kernel, side, grid, orbs),
        out_shape=jax.ShapeDtypeStruct((2, 1) + v_ext.shape, F32),
        in_specs=[pl.BlockSpec(memory_space=pltpu.HBM)] * 11,
        out_specs=pl.BlockSpec(memory_space=pltpu.VMEM),
        scratch_shapes=[
            vmem(2, side // 2, side),
            vmem(side // 2, side, dtype=jnp.int32),
            vmem(1, nproj, dtype=jnp.int32),
            vmem(nproj, nproj),
        ]
        + [pltpu.VMEM(t.shape, t.dtype) for t in consts]
        + [
            vmem(2 * nproj, count),
            vmem(*v_ext.shape),
            vmem(2 * nproj, count, dtype=BF16),
            vmem(2 * nproj, count, dtype=BF16),
            vmem(side // 2, ROWS * side),
        ]
        + [vmem(PLANES, grid * ROWS, side)] * 4
        + [
            vmem(2, PLANES, side, side),
            vmem(PLANES, side, side),
            vmem(PLANES, side, side),
            vmem(ROWS * ROWS, side),
            vmem(grid * ROWS, side),
            vmem(grid * ROWS, side),
            vmem(ROWS * ROWS, side),
            vmem(PLANES, ROWS, side),
            vmem(PLANES, side, side),
            vmem(2, 128),
            vmem(grid, 2, 128),
            vmem(2, side // 2, side),
            dma((11,)),
            dma((chunks,)), dma((chunks,)), dma((term_chunks,)), dma((term_chunks,)),
            dma, dma,
            dma((chunks,)), dma((chunks,)),
            dma, dma, dma, dma, dma, dma,
        ],
        compiler_params=pltpu.CompilerParams(
            collective_id=0, has_side_effects=True, vmem_limit_bytes=32 << 20
        ),
        name="hamiltonian",
    )(*[pltpu.with_memory_space_constraint(x, pltpu.HBM) for x in operands])


def solution(mesh):
    placed = (
        P(None, "orb", "grid"),
        P("grid"),
        P(None, None, "grid"),
        P(),
        P(),
        P("grid", None, None),
    )
    return jax.shard_map(
        functools.partial(body, mesh.shape["grid"], mesh.shape["orb"]),
        mesh=mesh,
        in_specs=placed,
        out_specs=P(None, "orb", "grid", None, None),
        check_vma=False,
    )
```

```python
import functools

import jax
import jax.numpy as jnp
import ml_dtypes
import numpy as np
from jax import lax
from jax.experimental import pallas as pl
from jax.experimental.pallas import tpu as pltpu
from jax.sharding import PartitionSpec as P

HARTREE_COUPLING = 256.0
F32, BF16 = jnp.float32, jnp.bfloat16
MESH = pl.DeviceIdType.MESH
HIGHEST = lax.Precision.HIGHEST
PLANES = 4
ROWS = 8
TERM_BEFORE = 3
TERM_AT = {"dens": (0,), "col": (1,), "idle": (2, 3), "ret": (2, 3)}


def halves(table):
    high = table.astype(ml_dtypes.bfloat16)
    low = (table - high.astype(np.float64)).astype(ml_dtypes.bfloat16)
    return np.stack([high, low])


def tables(side):
    grid = side // PLANES
    place = np.arange(side)

    def turn(first, second):
        angles = 2.0 * np.pi * ((first[:, None] * second[None, :]) % side) / side
        return np.cos(angles) / np.sqrt(side), np.sin(angles) / np.sqrt(side)

    expand = (np.arange(ROWS * side)[None, :] // ROWS == place[:, None]).astype(ml_dtypes.bfloat16)
    out_z = (PLANES * np.arange(grid)[None, :] + np.arange(PLANES)[:, None]).reshape(-1)
    in_z = (2 * np.arange(side // 2)[None, :] + np.arange(2)[:, None]).reshape(-1)
    cosine, sine = turn(out_z, in_z)
    z_table = np.block([[cosine, -sine], [sine, cosine]])
    cosine, sine = turn(place, place)
    y_table = np.block([[cosine, sine], [-sine, cosine]])
    cosine, sine = [t.reshape(side, grid, 1, PLANES) for t in turn(place, place)]
    x_table = np.concatenate(
        [np.concatenate([cosine, -sine], 2), np.concatenate([sine, cosine], 2)], 0
    ).reshape(2 * side, 2 * side)
    freq = (place + 1) // 2
    angles = 2.0 * np.pi * ((place[:, None] * freq[None, :]) % side) / side
    basis = np.where(place[None, :] % 2 == 1, np.cos(angles), np.sin(angles)) * np.sqrt(2.0 / side)
    basis[:, 0] = 1.0 / np.sqrt(side)
    basis[:, side - 1] = np.where(place % 2 == 0, 1.0, -1.0) / np.sqrt(side)
    spread = np.zeros((grid, ROWS, side))
    spread[:, :PLANES] = basis.reshape(grid, PLANES, side)
    spread = spread.reshape(grid * ROWS, side)
    real = np.concatenate([halves(basis), halves(basis.T)])
    return (
        expand,
        np.concatenate([halves(z_table), halves(y_table), halves(x_table)]),
        real,
        halves(spread.T),
        halves(spread),
    )


def split(values):
    high = values.astype(BF16)
    return high, (values - high.astype(F32)).astype(BF16)


def dot(left, right):
    return jnp.dot(left, right, preferred_element_type=F32)


def left_dot(table, first, values):
    high, low = split(values)
    return dot(table[first], high) + (dot(table[first], low) + dot(table[first + 1], high))


def right_dot(values, table, first):
    high, low = split(values)
    return dot(high, table[first]) + (dot(low, table[first]) + dot(high, table[first + 1]))


def turned_dot(left, right):
    return lax.dot_general(
        left, right, (((1,), (1,)), ((), ())), precision=HIGHEST, preferred_element_type=F32
    )


def kernel(
    side, grid, orbs,
    coef_hbm, gvec_hbm, atom_hbm, strength_hbm, expand_hbm, turn_hbm, real_hbm, zf_hbm, zb_hbm, proj_hbm, vext_hbm,
    out,
    coef, gvec, atom, strength, expand, turn, real, zfor, zback, proj, vext, proj_high, proj_low,
    mask, msg_c, msg_t, got_c, got_t, wave, dens_out, dens_in, col_out, col_in, ret_out, ret_in,
    pot_out, pot_in, dot_out, dot_in, nonlocal_rows,
    in_sem, send_c, recv_c, send_t, recv_t, send_dot, recv_dot, send_dens, recv_dens,
    send_col, recv_col, send_ret, recv_ret, send_pot, recv_pot,
):
    orb, place = lax.axis_index("orb"), lax.axis_index("grid")
    nproj = strength.shape[0]
    half = side // 2
    chunks, per = recv_c.shape[0], PLANES // recv_c.shape[0]
    term_chunks = recv_t.shape[0]

    loads = []
    for index, (source, target) in enumerate(
        [(gvec_hbm, gvec), (expand_hbm, expand), (coef_hbm, coef), (turn_hbm, turn), (proj_hbm, proj),
         (atom_hbm, atom), (strength_hbm, strength), (real_hbm, real), (zf_hbm, zfor), (zb_hbm, zback),
         (vext_hbm, vext)]
    ):
        loads.append(pltpu.make_async_copy(source, target, in_sem.at[index]))
        loads[-1].start()

    def over_grid(action):
        def step(k, carry):
            m = grid - k
            hop = jnp.where(m % 2 == 1, (m + 1) // 2, grid - m // 2)
            action(lax.rem(place + hop, grid))
            return carry

        lax.fori_loop(1, grid, step, 0)

    def over_orbs(action):
        def step(k, carry):
            action(lax.rem(orb + k, orbs))
            return carry

        lax.fori_loop(1, orbs, step, 0)

    def tile(index):
        return pl.ds(pl.multiple_of(index * ROWS, ROWS), ROWS)

    def planes_of(index):
        return pl.ds(pl.multiple_of(index * ROWS, ROWS), PLANES)

    def push(source, target, send_sem, recv_sem, device):
        pltpu.make_async_remote_copy(
            src_ref=source, dst_ref=target, send_sem=send_sem, recv_sem=recv_sem,
            device_id=device, device_id_type=MESH,
        ).start()

    def settle(ref, sem):
        pltpu.make_async_copy(ref, ref, sem).wait()

    def settle_rows(count, sem):
        settle(col_in.at[pl.ds(0, count), :], sem)

    col_in[...] = jnp.zeros_like(col_in)
    barrier = pltpu.get_barrier_semaphore()

    def greet(device):
        pl.semaphore_signal(barrier, inc=1, device_id=device, device_id_type=MESH)

    over_grid(lambda other: greet((orb, other)))
    over_orbs(lambda other: greet((other, place)))

    loads[0].wait()
    slot = gvec[...]
    iz, column = slot // (PLANES * side), slot % (PLANES * side)
    ix, iy = place * PLANES + column // side, column % side

    def frequency(index):
        return jnp.where(index < half, index, index - side).astype(F32)

    fx, fy, fz = frequency(ix), frequency(iy), frequency(iz)
    kinetic = 2.0 * (fx * fx + fy * fy + fz * fz) / (side * side)

    loads[1].wait()
    offset = (slot % ROWS).astype(F32).astype(BF16)
    wide_offset = dot(offset, expand[...])
    lane = lax.broadcasted_iota(jnp.int32, (half, ROWS * side), 1)
    mask[...] = jnp.where(wide_offset == (lane % ROWS).astype(F32), 1.0, 0.0)

    def fill_messages(real_part, imag_part, target):
        real_high, real_low = split(real_part)
        imag_high, imag_low = split(imag_part)
        wide = dot(jnp.concatenate([real_high, imag_high, real_low, imag_low], 0), expand[...])

        def slots(index):
            block = (wide[index * half:(index + 1) * half] * mask[...]).astype(BF16)
            return jnp.concatenate([block[:, : PLANES * side], block[:, PLANES * side:]], 0)

        high = jnp.concatenate([slots(0), slots(1)], 0)
        low = jnp.concatenate([slots(2), slots(3)], 0)
        sticks = dot(turn[0], high) + (dot(turn[0], low) + dot(turn[1], high))
        for x in range(PLANES):
            cols = slice(x * side, (x + 1) * side)
            lines = jnp.concatenate([sticks[:side, cols], sticks[side:, cols]], 1)
            lines = right_dot(lines, turn, 2)
            for plane in range(PLANES):
                for part in range(2):
                    target[plane, pl.ds(part * PLANES + x, grid, stride=ROWS), :] = lines[
                        plane * grid:(plane + 1) * grid, part * side:(part + 1) * side
                    ]

    loads[2].wait()
    loads[3].wait()
    fill_messages(coef[0], coef[1], msg_c)

    def send_planes(msg, got, chunk, send_sem, recv_sem):
        per = PLANES // send_sem.shape[0]
        planes = pl.ds(chunk * per, per)
        over_grid(
            lambda other: push(
                msg.at[planes, tile(other), :], got.at[planes, tile(place), :],
                send_sem.at[chunk], recv_sem.at[chunk], (orb, other),
            )
        )
        got[planes, tile(place), :] = msg[planes, tile(place), :]

    def all_but_one(ref, chunk, chunks):
        per = PLANES // chunks
        return ref.at[pl.ds(chunk * per, per), pl.ds(0, (grid - 1) * ROWS), :]

    loads[4].wait()

    def gather(row, carry):
        over_real, over_imag = carry
        cols = pl.ds(pl.multiple_of(row * side, side), side)
        c_real, c_imag = coef[0, pl.ds(row, 1), :], coef[1, pl.ds(row, 1), :]
        p_real, p_imag = proj[:nproj, cols], proj[nproj:, cols]
        return (
            over_real + (c_real * p_real + c_imag * p_imag),
            over_imag + (c_imag * p_real - c_real * p_imag),
        )

    zeros = jnp.zeros((nproj, side), F32)
    over_real, over_imag = lax.fori_loop(0, half, gather, (zeros, zeros), unroll=4)
    ones = jnp.ones((ROWS, side), F32)
    dot_out[...] = jnp.zeros_like(dot_out)
    power = coef[0] * coef[0] + coef[1] * coef[1]
    power = jnp.sum(power.reshape(half // ROWS, ROWS, side), axis=0)
    used = 2 * nproj + ROWS
    dot_out[0:1, 0:used] = turned_dot(ones, jnp.concatenate([over_real, over_imag, power], 0))[0:1]
    pl.semaphore_wait(barrier, grid + orbs - 2)
    over_grid(
        lambda other: push(dot_out, dot_in.at[place], send_dot, recv_dot, (orb, other))
    )
    dot_in[place] = dot_out[...]
    for chunk in range(chunks):
        send_planes(msg_c, got_c, chunk, send_c, recv_c)

    def halve(block, carry):
        cols = pl.ds(pl.multiple_of(block * ROWS * side, ROWS * side), ROWS * side)
        high, low = split(proj[:, cols])
        proj_high[:, cols] = high
        proj_low[:, cols] = low
        return carry

    lax.fori_loop(0, half // ROWS, halve, 0)

    loads[5].wait()
    loads[6].wait()
    settle(dot_in.at[pl.ds(0, grid - 1)], recv_dot)
    total = jnp.sum(dot_in[...], axis=0)
    mean = jnp.sum(total[:, 2 * nproj:used], axis=1, keepdims=True) / (side * side * side)
    row = lax.broadcasted_iota(jnp.int32, (ROWS, nproj), 0)
    both = jnp.where(row == 0, total[:, :nproj], total[:, nproj:2 * nproj])
    owner = jnp.broadcast_to(atom[...].astype(F32), (nproj, nproj))
    coupling = jnp.where(owner == owner.T, strength[...], 0.0)
    applied_high, applied_low = split(turned_dot(both, coupling))

    def spread(first):
        high, low = proj_high[first:first + nproj], proj_low[first:first + nproj]
        return dot(applied_high, high) + (dot(applied_high, low) + dot(applied_low, high))

    on_real, on_imag = spread(0), spread(nproj)
    term_real = on_real[0:1] - on_imag[1:2]
    term_imag = on_imag[0:1] + on_real[1:2]
    for r in range(half):
        nonlocal_rows[0, r:r + 1, :] = term_real[:, r * side:(r + 1) * side]
        nonlocal_rows[1, r:r + 1, :] = term_imag[:, r * side:(r + 1) * side]
    fill_messages(
        kinetic * coef[0] + nonlocal_rows[0], kinetic * coef[1] + nonlocal_rows[1], msg_t
    )

    def send_term(moment):
        for chunk in TERM_AT.get(moment, ()):
            send_planes(msg_t, got_t, chunk, send_t, recv_t)

    for index in (7, 8, 9, 10):
        loads[index].wait()
    for chunk in range(chunks):
        planes = range(chunk * per, (chunk + 1) * per)
        settle(all_but_one(got_c, chunk, chunks), recv_c.at[chunk])
        send_term("wave%d" % chunk)
        field = left_dot(turn, 4, jnp.concatenate([got_c[p] for p in planes], 1))
        density = field[:side] * field[:side] + field[side:] * field[side:] - mean
        for k, p in enumerate(planes):
            wave[0, p] = field[:side, k * side:(k + 1) * side]
            wave[1, p] = field[side:, k * side:(k + 1) * side]
        modes = left_dot(real, 2, density)
        for k, p in enumerate(planes):
            dens_out[p] = modes[:, k * side:(k + 1) * side]
        span = pl.ds(chunk * per, per)
        over_orbs(
            lambda other: push(
                dens_out.at[span, tile(other), :], dens_in.at[span, tile(orb), :],
                send_dens.at[chunk], recv_dens.at[chunk], (other, place),
            )
        )
        dens_in[span, tile(orb), :] = dens_out[span, tile(orb), :]

    send_term("dens")

    stride = grid // ROWS
    shift = lax.rem(orb, stride)
    my_row = place // stride
    is_owner = lax.rem(place, stride) == shift

    col_out[...] = jnp.zeros_like(col_out)
    sums = []
    for chunk in range(chunks):
        span = pl.ds(chunk * per, per)
        settle(dens_in.at[span, pl.ds(0, (orbs - 1) * ROWS), :], recv_dens.at[chunk])
        for p in range(chunk * per, (chunk + 1) * per):
            summed = dens_in[p, 0:ROWS, :]
            for o in range(1, orbs):
                summed = summed + dens_in[p, o * ROWS:(o + 1) * ROWS, :]
            sums.append(summed)
    modes = right_dot(jnp.concatenate(sums, 0), real, 0)
    for p in range(PLANES):
        col_out[pl.ds(p, ROWS, stride=ROWS), :] = modes[p * ROWS:(p + 1) * ROWS]

    def send_column(row_index, carry):
        target = row_index * stride + shift

        @pl.when(target != place)
        def _():
            push(
                col_out.at[planes_of(row_index), :], col_in.at[planes_of(place), :],
                send_col, recv_col, (orb, target),
            )

        return carry

    lax.fori_loop(0, ROWS, send_column, 0)
    send_term("col")

    @pl.when(is_owner)
    def _():
        col_in[tile(place), :] = col_out[tile(my_row), :]
        settle_rows((grid - 1) * PLANES, recv_col)
        kx = (orb * ROWS + my_row + 1) // 2
        kz = (lax.broadcasted_iota(jnp.int32, (side, side), 0) + 1) // 2
        ky = (lax.broadcasted_iota(jnp.int32, (side, side), 1) + 1) // 2
        squared = (kx * kx + ky * ky + kz * kz).astype(F32)
        coulomb = jnp.where(squared > 0, HARTREE_COUPLING / jnp.maximum(squared, 1.0), 0.0)
        spectrum = left_dot(zfor, 0, col_in[...]) * coulomb
        ret_out[...] = left_dot(zback, 0, spectrum)
        over_grid(
            lambda other: push(
                ret_out.at[planes_of(other), :], ret_in.at[planes_of(my_row), :],
                send_ret, recv_ret, (orb, other),
            )
        )
        ret_in[tile(my_row), :] = ret_out[tile(place), :]
        send_term("ret")
        settle_rows((ROWS - 1) * PLANES, recv_ret)
        settle_rows((grid - 1) * PLANES, send_ret)
        settle_rows((ROWS - 1) * PLANES, send_col)

    @pl.when(jnp.logical_not(is_owner))
    def _():
        send_term("idle")
        settle_rows(ROWS * PLANES, recv_ret)
        settle_rows(ROWS * PLANES, send_col)

    rows = jnp.concatenate([ret_in[pl.ds(p, ROWS, stride=ROWS), :] for p in range(PLANES)], 0)
    rows = right_dot(rows, real, 2)
    for p in range(PLANES):
        pot_out[p] = rows[p * ROWS:(p + 1) * ROWS]
    over_orbs(
        lambda other: push(
            pot_out, pot_in.at[:, tile(orb), :], send_pot, recv_pot, (other, place)
        )
    )
    pot_in[:, tile(orb), :] = pot_out[...]
    send_term("pot")

    per_term = PLANES // term_chunks

    def term_in_space(chunk):
        planes = range(chunk * per_term, (chunk + 1) * per_term)
        settle(all_but_one(got_t, chunk, term_chunks), recv_t.at[chunk])
        field = left_dot(turn, 4, jnp.concatenate([got_t[p] for p in planes], 1))
        for k, p in enumerate(planes):
            out[0, 0, p] = field[:side, k * side:(k + 1) * side]
            out[1, 0, p] = field[side:, k * side:(k + 1) * side]

    for chunk in range(TERM_BEFORE):
        term_in_space(chunk)
    settle(pot_in.at[:, pl.ds(0, (orbs - 1) * ROWS), :], recv_pot)
    hartree = left_dot(real, 0, jnp.concatenate([pot_in[p] for p in range(PLANES)], 1))
    for p in range(PLANES):
        vext[p] = vext[p] + hartree[:, p * side:(p + 1) * side]
    for chunk in range(term_chunks):
        if chunk >= TERM_BEFORE:
            term_in_space(chunk)
        for p in range(chunk * per_term, (chunk + 1) * per_term):
            out[0, 0, p] = out[0, 0, p] + vext[p] * wave[0, p]
            out[1, 0, p] = out[1, 0, p] + vext[p] * wave[1, p]

    for chunk in range(chunks):
        settle(all_but_one(msg_c, chunk, chunks), send_c.at[chunk])
        span = pl.ds(chunk * per, per)
        settle(dens_out.at[span, pl.ds(0, (orbs - 1) * ROWS), :], send_dens.at[chunk])
    for chunk in range(term_chunks):
        settle(all_but_one(msg_t, chunk, term_chunks), send_t.at[chunk])
    settle(dot_in.at[pl.ds(0, grid - 1)], send_dot)
    settle(pot_in.at[:, pl.ds(0, (orbs - 1) * ROWS), :], send_pot)


def body(grid, orbs, coeffs, gvec_map, projectors, proj_atom, proj_strength, v_ext):
    side = v_ext.shape[1]
    nproj = proj_strength.shape[0]
    count = coeffs.shape[2]
    chunks, term_chunks = 2, 4
    consts = [jnp.asarray(t) for t in tables(side)]
    dma = pltpu.SemaphoreType.DMA

    def vmem(*shape, dtype=F32):
        return pltpu.VMEM(shape, dtype)

    operands = [
        coeffs.reshape(2, side // 2, side),
        gvec_map.reshape(side // 2, side),
        proj_atom.reshape(1, nproj),
        proj_strength,
        *consts,
        projectors.reshape(2 * nproj, count),
        v_ext,
    ]
    return pl.pallas_call(
        functools.partial(kernel, side, grid, orbs),
        out_shape=jax.ShapeDtypeStruct((2, 1) + v_ext.shape, F32),
        in_specs=[pl.BlockSpec(memory_space=pltpu.HBM)] * 11,
        out_specs=pl.BlockSpec(memory_space=pltpu.VMEM),
        scratch_shapes=[
            vmem(2, side // 2, side),
            vmem(side // 2, side, dtype=jnp.int32),
            vmem(1, nproj, dtype=jnp.int32),
            vmem(nproj, nproj),
        ]
        + [pltpu.VMEM(t.shape, t.dtype) for t in consts]
        + [
            vmem(2 * nproj, count),
            vmem(*v_ext.shape),
            vmem(2 * nproj, count, dtype=BF16),
            vmem(2 * nproj, count, dtype=BF16),
            vmem(side // 2, ROWS * side),
        ]
        + [vmem(PLANES, grid * ROWS, side)] * 4
        + [
            vmem(2, PLANES, side, side),
            vmem(PLANES, side, side),
            vmem(PLANES, side, side),
            vmem(ROWS * ROWS, side),
            vmem(grid * ROWS, side),
            vmem(grid * ROWS, side),
            vmem(ROWS * ROWS, side),
            vmem(PLANES, ROWS, side),
            vmem(PLANES, side, side),
            vmem(1, 128),
            vmem(grid, 1, 128),
            vmem(2, side // 2, side),
            dma((11,)),
            dma((chunks,)), dma((chunks,)), dma((term_chunks,)), dma((term_chunks,)),
            dma, dma,
            dma((chunks,)), dma((chunks,)),
            dma, dma, dma, dma, dma, dma,
        ],
        compiler_params=pltpu.CompilerParams(
            collective_id=0, has_side_effects=True, vmem_limit_bytes=32 << 20
        ),
        name="hamiltonian",
    )(*[pltpu.with_memory_space_constraint(x, pltpu.HBM) for x in operands])


def solution(mesh):
    placed = (
        P(None, "orb", "grid"),
        P("grid"),
        P(None, None, "grid"),
        P(),
        P(),
        P("grid", None, None),
    )
    return jax.shard_map(
        functools.partial(body, mesh.shape["grid"], mesh.shape["orb"]),
        mesh=mesh,
        in_specs=placed,
        out_specs=P(None, "orb", "grid", None, None),
        check_vma=False,
    )
```
